32 devices in a mesh: groups: 2 (over x), owner: 16 (over z, y, core).
Axes of the slice: x: 2, y: 2, z: 4, core: 2. Of those that a mesh axis runs over, the one named last changes fastest.
Arguments:
- states: bfloat16 [832, 8192], P(('groups', 'owner')), parts along dimension 0, may hold values from -6 to 6
- row_adapter_index: int32 [832], P('groups'), parts along dimension 0, may hold values from 0 to 63, as said below
- adapter_storage_slot: int32 [128], P('groups'), parts along dimension 0, may hold values from 0 to 63, as said below
- base_weight: bfloat16 [8192, 8192], P(None, 'owner'), may hold values from -0.0625 to 0.0625
- down_weight: bfloat16 [64, 8192, 64], P('owner'), may hold values from -0.0625 to 0.0625
- up_weight: bfloat16 [64, 64, 8192], P('owner'), may hold values from -0.75 to 0.75
Outputs:
- layer_out: bfloat16 [832, 8192], P(('groups', 'owner')), parts along dimension 0
The draws below stay inside these ranges and needn't reach their ends.
There are 2 independent parts, one for each index of `groups`. The reference program is written for one: setup_inputs(seed, part) draws one part's arguments, and reference() takes and returns one part's arrays. A program takes and returns all parts, laid end to end along the dimension named above; an argument that names none is the same for every part. Nothing has to cross between parts.
Inputs may be any that keep to these rules, and one draw needn't show every extreme that they name: `adapter_storage_slot`: a permutation of 0 to 63. With owner(r) = adapter_storage_slot[row_adapter_index[r]] // 4, the 26 rows of one row group (aligned blocks) name at most 2 rows of one owner; in every draw some owner gets exactly 2 rows from every row group.
All inputs are finite; a program needn't handle non-finite values.
Results may differ from the reference program's by a relative error of at most 0.0053.
Values may be sent and summed in bfloat16 or wider, within the bound.
No kernel may reach another device: no remote copies, remote signals or barrier semaphores. Data moves between devices by JAX's collectives and lax.ppermute only.
A program may use at most 192 MiB of HBM per device.

```python
import jax
import jax.numpy as jnp
from jax import lax

MODEL_WIDTH = 8192
ADAPTER_RANK = 64
ADAPT_DEV = 4
OWNER_ROW_LIMIT = 2
ROWS_DEV = 26
ROWS = 416
ADAPTER_TOTAL = 64
N_OWNER = 16


def slot_table(key):
    return jax.random.permutation(key, ADAPTER_TOTAL).astype(jnp.int32)


def draw_adapter_storage_slot(key, part):
    table = slot_table(key)
    return table


def draw_row_adapter_index(key, part):
    table = slot_table(key)
    key = jax.random.fold_in(key, 23)
    inverse = jnp.argsort(table).astype(jnp.int32)
    key_hot, key_blocks, key_local = jax.random.split(key, 3)
    hot_owner = jax.random.randint(key_hot, (), 0, N_OWNER).astype(jnp.int32)
    block_keys = jax.random.split(key_blocks, N_OWNER)

    def one_group(block_key):
        key_spread, key_order = jax.random.split(block_key)
        spread = jax.random.permutation(key_spread, OWNER_ROW_LIMIT * (N_OWNER - 1))[:ROWS_DEV - OWNER_ROW_LIMIT] // OWNER_ROW_LIMIT
        others = (hot_owner + 1 + spread.astype(jnp.int32)) % N_OWNER
        owners_block = jnp.concatenate([jnp.full((OWNER_ROW_LIMIT,), hot_owner, jnp.int32), others.astype(jnp.int32)])
        order = jax.random.permutation(key_order, ROWS_DEV)
        return owners_block[order]
    owners_all = jax.vmap(one_group)(block_keys).reshape(ROWS)
    local_pick = jax.random.randint(key_local, (ROWS,), 0, ADAPT_DEV).astype(jnp.int32)
    slots = owners_all * ADAPT_DEV + local_pick
    return inverse[slots].astype(jnp.int32)


def block_levels(rng, extent, cuts, low, high):
    factor_of = 1.0
    for dim, parts in cuts:
        heights = jax.random.uniform(jax.random.fold_in(jax.random.fold_in(rng, 6), dim), (parts,), jnp.float32, low / len(cuts), high / len(cuts))
        factor_of = factor_of * jnp.repeat(jnp.exp(heights), extent[dim] // parts).reshape((-1,) + (1,) * (len(extent) - 1 - dim))
    return factor_of


def centred(own_key, dims, scale, limit, cuts=(), dtype=jnp.bfloat16):
    result = scale * jax.random.normal(own_key, dims, jnp.float32)
    if cuts:
        result = result * block_levels(own_key, dims, cuts, -0.22, 0.18)
    return jnp.clip(result, -limit, limit).astype(dtype)


def setup_inputs(seed: int = 0, part: int = 0) -> dict:
    key_list = jax.random.split(jax.random.key(seed), 7)
    part_keys = jax.random.split(jax.random.fold_in(key_list[6], part), 7)
    states = centred(part_keys[0], (ROWS, MODEL_WIDTH), 1.0, 6.0, ((0, 16),))
    row_adapter_index = draw_row_adapter_index(jax.random.fold_in(jax.random.fold_in(key_list[6], part), 71), part)
    adapter_storage_slot = draw_adapter_storage_slot(jax.random.fold_in(jax.random.fold_in(key_list[6], part), 71), part)
    base_weight = centred(key_list[3], (MODEL_WIDTH, MODEL_WIDTH), MODEL_WIDTH ** -0.5, 0.0625, ((1, 16),))
    down_weight = centred(key_list[4], (ADAPTER_TOTAL, MODEL_WIDTH, ADAPTER_RANK), MODEL_WIDTH ** -0.5, 0.0625, ((0, 16),))
    up_weight = centred(key_list[5], (ADAPTER_TOTAL, ADAPTER_RANK, MODEL_WIDTH), ADAPTER_RANK ** -0.5, 0.75, ((0, 16),))
    return dict(states=states, row_adapter_index=row_adapter_index, adapter_storage_slot=adapter_storage_slot, base_weight=base_weight, down_weight=down_weight, up_weight=up_weight)


adapter_scale = 0.5


def reference(states, row_adapter_index, adapter_storage_slot, base_weight, down_weight, up_weight):
    base_output = jnp.dot(states, base_weight, preferred_element_type=jnp.float32).astype(jnp.bfloat16)
    slot_per_row = jnp.take(adapter_storage_slot, row_adapter_index).astype(jnp.int32)

    def down_rank(pair):
        input_vector, storage_position = pair
        return jnp.dot(input_vector, down_weight[storage_position], preferred_element_type=jnp.float32)

    rank_projection = lax.map(down_rank, (states, slot_per_row)).astype(jnp.bfloat16)

    def rank_expanded(pair):
        input_vector, storage_position = pair
        return jnp.dot(input_vector, up_weight[storage_position], preferred_element_type=jnp.float32)

    adapter_delta = lax.map(rank_expanded, (rank_projection, slot_per_row)).astype(jnp.bfloat16)
    base_output = lax.optimization_barrier(base_output)
    adapter_delta = lax.optimization_barrier(adapter_delta)
    total_output = base_output.astype(jnp.float32) + adapter_scale * adapter_delta.astype(jnp.float32)
    return total_output.astype(jnp.bfloat16)
```

```python
import functools

import jax
import jax.numpy as jnp
import numpy as np
from jax import lax
from jax.experimental import pallas as pl
from jax.experimental.pallas import tpu as pltpu
from jax.sharding import PartitionSpec as P

OWNER_ROW_LIMIT = 2
ROW_PAD = 16
adapter_scale = 0.5

VMEM = pl.BlockSpec(memory_space=pltpu.VMEM)
SMEM = pl.BlockSpec(memory_space=pltpu.SMEM)
ANY = pl.BlockSpec(memory_space=pl.ANY)
MIB = 1 << 20


def ring_order(chips):
    return list(range(0, chips, 2)) + list(range(1, chips, 2))[::-1]


def ring_tables(owner_count):
    chips = owner_count // 2
    order = ring_order(chips)
    place = {chip: at for at, chip in enumerate(order)}

    def beside(chip, core, hops):
        return order[(place[chip] + (-hops if core == 0 else hops)) % chips]

    step = [
        (2 * chip + core, 2 * order[(place[chip] + (1 if core == 0 else -1)) % chips] + core)
        for chip in range(chips)
        for core in range(2)
    ]
    swap = [(device, device ^ 1) for device in range(owner_count)]
    sources = np.zeros((owner_count, owner_count), np.int32)
    for device in range(owner_count):
        chip, core = divmod(device, 2)
        row = [device, device ^ 1]
        for hops in range(1, chips // 2 + 1):
            mine, mates = beside(chip, core, hops), beside(chip, 1 - core, hops)
            row += [2 * mine + core, 2 * mates + 1 - core]
            if 2 * hops < chips:
                row += [2 * mine + 1 - core, 2 * mates + core]
        assert sorted(row) == list(range(owner_count))
        sources[device] = row
    return step, swap, sources


def pair_rows(x):
    rows, width = x.shape

    def kernel(x_ref, o_ref):
        o_ref[...] = x_ref[...].reshape(rows // 2, 2, width)

    return pl.pallas_call(
        kernel,
        out_shape=jax.ShapeDtypeStruct((rows // 2, 2, width), x.dtype),
        in_specs=[VMEM],
        out_specs=VMEM,
        compiler_params=pltpu.CompilerParams(vmem_limit_bytes=4 * MIB),
        name="pair_rows",
    )(x)


def hold(*weights):
    def kernel(*refs):
        n = len(weights)
        sem = refs[2 * n]
        copies = [
            pltpu.make_async_copy(refs[i], refs[n + i], sem.at[i]) for i in range(n)
        ]
        for copy in copies:
            copy.start()
        for copy in copies:
            copy.wait()

    return pl.pallas_call(
        kernel,
        out_shape=[pltpu.VMEM(w.shape, w.dtype) for w in weights],
        in_specs=[ANY] * len(weights),
        out_specs=[VMEM] * len(weights),
        scratch_shapes=[pltpu.SemaphoreType.DMA((len(weights),))],
        compiler_params=pltpu.CompilerParams(vmem_limit_bytes=1 * MIB),
        name="hold",
    )(*weights)


def block_products(sources, code, blocks, base_weight, down, up, rank, owner_count):
    count = len(blocks)
    pairs, _, width = blocks[0].shape
    rows = 2 * pairs
    padded = -(-rows // ROW_PAD) * ROW_PAD
    columns = base_weight.shape[1]
    ranks = down.shape[0]
    depth = min(width, 1024)

    def kernel(src_ref, code_ref, *refs):
        block_refs = refs[:count]
        w_ref, d_ref, u_ref, out_ref, x_ref = refs[count:]
        for b in range(count):
            x_ref[padded * b : padded * b + rows] = block_refs[b][...].reshape(rows, width)
            x_ref[padded * b + rows : padded * (b + 1)] = jnp.zeros(
                (padded - rows, width), x_ref.dtype
            )
        low = jnp.zeros((padded * count, ranks), jnp.float32)
        for at in range(0, width, depth):
            low += lax.dot_general(
                x_ref[:, at : at + depth],
                d_ref[:, at : at + depth],
                (((1,), (1,)), ((), ())),
                preferred_element_type=jnp.float32,
            )
        low = low.astype(jnp.bfloat16).astype(jnp.float32)
        adapter = lax.broadcasted_iota(jnp.int32, (padded, ranks), 1) // rank
        chosen = []
        for b in range(count):
            row_code = code_ref[src_ref[b]]
            for q in range(OWNER_ROW_LIMIT):
                mask = row_code == OWNER_ROW_LIMIT * adapter + q
                chosen.append(
                    jnp.sum(
                        jnp.where(mask, low[padded * b : padded * (b + 1)], 0.0),
                        axis=0,
                        keepdims=True,
                    )
                )
        chosen = jnp.concatenate(chosen, axis=0).astype(jnp.bfloat16)
        base = jnp.zeros((padded * count, columns), jnp.float32)
        for at in range(0, width, depth):
            base += jnp.dot(
                x_ref[:, at : at + depth],
                w_ref[at : at + depth, :],
                preferred_element_type=jnp.float32,
            )
        for b in range(count):
            out_ref[b, :pairs] = (
                base[padded * b : padded * b + rows]
                .astype(jnp.bfloat16)
                .reshape(pairs, 2, columns)
            )
        for k in range(owner_count):
            delta = jnp.dot(
                chosen, u_ref[:, columns * k : columns * (k + 1)], preferred_element_type=jnp.float32
            ).astype(jnp.bfloat16)
            for b in range(count):
                out_ref[b, pairs + k] = delta[OWNER_ROW_LIMIT * b : OWNER_ROW_LIMIT * (b + 1)]

    return pl.pallas_call(
        kernel,
        out_shape=jax.ShapeDtypeStruct((count, pairs + owner_count, 2, columns), jnp.bfloat16),
        in_specs=[SMEM, VMEM] + [VMEM] * (count + 3),
        out_specs=VMEM,
        scratch_shapes=[pltpu.VMEM((padded * count, width), jnp.bfloat16)],
        compiler_params=pltpu.CompilerParams(vmem_limit_bytes=16 * MIB),
        cost_estimate=pl.CostEstimate(
            flops=2 * padded * count * width * (columns + ranks),
            bytes_accessed=width * (columns + 2 * ranks) * 2,
            transcendentals=0,
        ),
        name="block_products",
    )(sources, code, *blocks, base_weight, down, up)


def pack(sources, pieces, owner_count):
    counts = [p.shape[0] for p in pieces]

    def kernel(src_ref, *refs):
        piece_refs, out_ref, sem = refs[: len(pieces)], refs[-2], refs[-1]
        copies = []
        at = 0
        for ref, count in zip(piece_refs, counts):
            for b in range(count):
                copies.append(
                    pltpu.make_async_copy(ref.at[b], out_ref.at[src_ref[at]], sem.at[at])
                )
                at += 1
        for copy in copies:
            copy.start()
        for copy in copies:
            copy.wait()

    return pl.pallas_call(
        kernel,
        out_shape=jax.ShapeDtypeStruct((owner_count,) + pieces[0].shape[1:], pieces[0].dtype),
        in_specs=[SMEM] + [ANY] * len(pieces),
        out_specs=ANY,
        scratch_shapes=[pltpu.SemaphoreType.DMA((owner_count,))],
        compiler_params=pltpu.CompilerParams(vmem_limit_bytes=1 * MIB),
        name="pack",
    )(sources, *pieces)


def assemble(key, received, rows):
    owner_count, _, _, columns = received.shape
    pairs = rows // 2
    slots = OWNER_ROW_LIMIT * owner_count

    def kernel(key_ref, r_ref, o_ref):
        pick = (
            key_ref[...] == lax.broadcasted_iota(jnp.int32, (rows, slots), 1)
        ).astype(jnp.bfloat16)
        for k in range(owner_count):
            delta = jnp.dot(
                pick,
                r_ref[:, pairs + k].reshape(slots, columns),
                preferred_element_type=jnp.float32,
            )
            base = r_ref[k, :pairs].reshape(rows, columns).astype(jnp.float32)
            o_ref[:, columns * k : columns * (k + 1)] = (base + adapter_scale * delta).astype(
                o_ref.dtype
            )

    return pl.pallas_call(
        kernel,
        out_shape=jax.ShapeDtypeStruct((rows, owner_count * columns), jnp.bfloat16),
        in_specs=[VMEM, VMEM],
        out_specs=VMEM,
        compiler_params=pltpu.CompilerParams(vmem_limit_bytes=16 * MIB),
        name="assemble",
    )(key, received)


def per_device(
    states, row_adapter_index, adapter_storage_slot, base_weight, down_weight, up_weight
):
    owner_count = lax.axis_size("owner")
    me = lax.axis_index("owner")
    rows, width = states.shape
    adapters, rank = down_weight.shape[0], down_weight.shape[2]
    padded = -(-rows // ROW_PAD) * ROW_PAD
    step, swap, sources = ring_tables(owner_count)
    send = functools.partial(lax.ppermute, axis_name="owner")

    down = down_weight.transpose(0, 2, 1).reshape(adapters * rank, width)
    up = up_weight.reshape(adapters * rank, width)
    held = hold(base_weight, down, up)

    index = row_adapter_index.reshape(owner_count, rows)
    total = adapter_storage_slot.shape[0]
    slot = jnp.sum(
        jnp.where(
            index[:, :, None] == jnp.arange(total, dtype=jnp.int32),
            adapter_storage_slot,
            0,
        ),
        axis=2,
    )
    owner = slot // adapters
    earlier = jnp.arange(rows)[None, :] < jnp.arange(rows)[:, None]
    position = jnp.sum(
        ((owner[:, :, None] == owner[:, None, :]) & earlier).astype(jnp.int32), axis=2
    )
    code = jnp.where(owner == me, (slot - owner * adapters) * OWNER_ROW_LIMIT + position, -1)
    code = jnp.pad(code, ((0, 0), (0, padded - rows)), constant_values=-1)[:, :, None]
    key = lax.dynamic_index_in_dim(owner * OWNER_ROW_LIMIT + position, me, 0, False)[:, None]
    mine = lax.dynamic_index_in_dim(jnp.asarray(sources), me, 0, False)

    own = pair_rows(states)
    mate = send(own, perm=swap)
    groups = [[own, mate]]
    first, second = own, mate
    chips = owner_count // 2
    for hops in range(1, chips // 2 + 1):
        first = send(first, perm=step)
        group = [first, send(first, perm=swap)]
        if 2 * hops < chips:
            second = send(second, perm=step)
            group += [second, send(second, perm=swap)]
        groups.append(group)
    pieces = []
    at = 0
    for group in groups:
        pieces.append(
            block_products(
                mine[at : at + len(group)], code, group, *held, rank, owner_count
            )
        )
        at += len(group)
    packed = pack(mine, pieces, owner_count)
    received = lax.all_to_all(packed, "owner", split_axis=0, concat_axis=0, tiled=True)
    return assemble(key, received, rows)


def solution(mesh):
    return jax.shard_map(
        per_device,
        mesh=mesh,
        in_specs=(
            P(("groups", "owner"), None),
            P("groups"),
            P("groups"),
            P(None, "owner"),
            P("owner", None, None),
            P("owner", None, None),
        ),
        out_specs=P(("groups", "owner"), None),
        check_vma=False,
    )
```

```python
import functools

import jax
import jax.numpy as jnp
import numpy as np
from jax import lax
from jax.experimental import pallas as pl
from jax.experimental.pallas import tpu as pltpu
from jax.sharding import PartitionSpec as P

OWNER_ROW_LIMIT = 2
ROW_PAD = 16
adapter_scale = 0.5

VMEM = pl.BlockSpec(memory_space=pltpu.VMEM)
SMEM = pl.BlockSpec(memory_space=pltpu.SMEM)
ANY = pl.BlockSpec(memory_space=pl.ANY)
MIB = 1 << 20


def ring_order(chips):
    return list(range(0, chips, 2)) + list(range(1, chips, 2))[::-1]


def ring_tables(owner_count):
    chips = owner_count // 2
    order = ring_order(chips)
    place = {chip: at for at, chip in enumerate(order)}

    def beside(chip, hops):
        return order[(place[chip] + hops) % chips]

    def turned(hops):
        return [
            (2 * chip + core, 2 * beside(chip, -hops if core else hops) + core)
            for chip in range(chips)
            for core in range(2)
        ]

    swap = [(device, device ^ 1) for device in range(owner_count)]
    sources = np.zeros((2, owner_count, owner_count), np.int32)
    for device in range(owner_count):
        chip, core = divmod(device, 2)
        blocks, pieces = [device, device ^ 1], [[device, device ^ 1]]
        for hops in range(1, chips // 2 + 1):
            mine = 2 * beside(chip, hops if core else -hops)
            mates = 2 * beside(chip, -hops if core else hops)
            if 2 * hops < chips:
                blocks += [mine + core, mates + 1 - core, mine + 1 - core, mates + core]
                pieces += [[mates + core, mine + 1 - core], [mine + core, mates + 1 - core]]
            else:
                blocks += [mine + core, mates + 1 - core]
                pieces += [[mine + core, mine + 1 - core]]
        assert sorted(blocks) == sorted(sum(pieces, [])) == list(range(owner_count))
        sources[0, device], sources[1, device] = blocks, sum(pieces, [])
    return turned, swap, sources


def pair_rows(x):
    rows, width = x.shape

    def kernel(x_ref, o_ref):
        o_ref[...] = x_ref[...].reshape(rows // 2, 2, width)

    return pl.pallas_call(
        kernel,
        out_shape=jax.ShapeDtypeStruct((rows // 2, 2, width), x.dtype),
        in_specs=[VMEM],
        out_specs=VMEM,
        compiler_params=pltpu.CompilerParams(vmem_limit_bytes=4 * MIB),
        name="pair_rows",
    )(x)


def row_places(row_adapter_index, adapter_storage_slot, rows, adapters):
    total, slots = row_adapter_index.shape[0], adapter_storage_slot.shape[0]

    def kernel(index_ref, table_ref, o_ref):
        adapter = lax.broadcasted_iota(jnp.int32, (slots, total), 0)
        slot = jnp.sum(
            jnp.where(adapter == index_ref[...], table_ref[...], 0), axis=0, keepdims=True
        )
        owner = slot // adapters
        at = lax.broadcasted_iota(jnp.int32, (1, total), 1) % rows
        earlier = jnp.zeros_like(slot)
        for back in range(1, rows):
            same = (pltpu.roll(owner, back, 1) == owner) & (at >= back)
            earlier += same.astype(jnp.int32)
        place = slot * OWNER_ROW_LIMIT + earlier
        for group in range(total // rows):
            o_ref[group : group + 1] = place[:, group * rows : (group + 1) * rows]

    return pl.pallas_call(
        kernel,
        out_shape=jax.ShapeDtypeStruct((total // rows, rows), jnp.int32),
        in_specs=[VMEM, VMEM],
        out_specs=VMEM,
        compiler_params=pltpu.CompilerParams(vmem_limit_bytes=8 * MIB),
        name="row_places",
    )(row_adapter_index.reshape(1, total), adapter_storage_slot.reshape(slots, 1))


def hold(weight, carry, before, turn=False):
    shape = weight.shape[::-1] if turn else weight.shape
    parts = 8

    def kernel(*refs):
        src, dst, sem = refs[0], refs[2 + len(before)], refs[-1]
        landing = refs[-2] if turn else dst
        copies = []
        size = weight.shape[1 if turn else 0] // parts
        spans = [pl.ds(part * size, size) for part in range(parts)]
        for part, span in enumerate(spans):
            at = (slice(None), span) if turn else (span,)
            copies.append(pltpu.make_async_copy(src.at[at], landing.at[at], sem.at[part]))
        for copy in copies:
            copy.start()
        for copy, span in zip(copies, spans):
            copy.wait()
            if turn:
                dst[span, :] = landing[:, span].T

    return pl.pallas_call(
        kernel,
        out_shape=[
            pltpu.VMEM(shape, weight.dtype),
            jax.ShapeDtypeStruct(carry.shape, carry.dtype),
        ],
        in_specs=[ANY] * (2 + len(before)),
        out_specs=[VMEM, ANY],
        input_output_aliases={1: 1},
        scratch_shapes=([pltpu.VMEM(weight.shape, weight.dtype)] if turn else [])
        + [pltpu.SemaphoreType.DMA((parts,))],
        compiler_params=pltpu.CompilerParams(vmem_limit_bytes=(8 if turn else 1) * MIB),
        name="hold",
    )(weight, carry, *before)


def after(x, before):
    def kernel(*refs):
        pass

    return pl.pallas_call(
        kernel,
        out_shape=jax.ShapeDtypeStruct(x.shape, x.dtype),
        in_specs=[ANY] * (1 + len(before)),
        out_specs=ANY,
        input_output_aliases={0: 0},
        compiler_params=pltpu.CompilerParams(vmem_limit_bytes=1 * MIB),
        name="after",
    )(x, *before)


def block_products(sources, start, row_place, blocks, places, weights, rank, owner_count):
    base_weight, down, up = weights
    count = len(blocks)
    results = 1 + max(result for result, _ in places)
    pairs, _, width = blocks[0].shape
    rows = 2 * pairs
    padded = -(-rows // ROW_PAD) * ROW_PAD
    columns = base_weight.shape[1]
    ranks = down.shape[1]
    depth = min(width, 1024)
    parts = width // depth
    adapters = ranks // rank
    taken = OWNER_ROW_LIMIT * adapters
    takes = -(-OWNER_ROW_LIMIT * count // 8) * 8

    def kernel(src_ref, place_ref, *refs):
        me = lax.axis_index("owner")
        block_refs = refs[:count]
        w_ref, d_ref, u_ref = refs[count : count + 3]
        out_refs = refs[count + 3 :][:results]
        x_ref, code_ref = refs[-2:]
        for b in range(count):
            x_ref[padded * b : padded * b + rows] = block_refs[b][...].reshape(rows, width)
            x_ref[padded * b + rows : padded * (b + 1)] = jnp.zeros(
                (padded - rows, width), x_ref.dtype
            )
        low = jnp.zeros((padded * count, ranks), jnp.float32)
        for part in range(parts):
            at = part * depth
            low += jnp.dot(
                x_ref[:, at : at + depth],
                d_ref[at : at + depth, :],
                preferred_element_type=jnp.float32,
            )
        low = low.astype(jnp.bfloat16)
        code_ref[...] = jnp.full_like(code_ref, -1)
        for b in range(count):
            code_ref[:, padded * b : padded * b + rows] = (
                place_ref[pl.ds(src_ref[me, start + b], 1), :] - me * taken
            )
        row = lax.broadcasted_iota(jnp.int32, (adapters * takes, padded * count), 0)
        lane = lax.broadcasted_iota(jnp.int32, (adapters * takes, padded * count), 1)
        place = row % takes
        wanted = row // takes * OWNER_ROW_LIMIT + place % OWNER_ROW_LIMIT
        match = (code_ref[...] == wanted) & (lane // padded == place // OWNER_ROW_LIMIT)
        found = jnp.dot(match.astype(jnp.bfloat16), low, preferred_element_type=jnp.float32)
        adapter = lax.broadcasted_iota(jnp.int32, (takes, ranks), 1) // rank
        chosen = jnp.zeros((takes, ranks), jnp.float32)
        for a in range(adapters):
            chosen = jnp.where(adapter == a, found[takes * a : takes * (a + 1)], chosen)
        chosen = chosen.astype(jnp.bfloat16)
        base = jnp.zeros((padded * count, columns), jnp.float32)
        for part in range(parts):
            at = part * depth
            base += jnp.dot(
                x_ref[:, at : at + depth],
                w_ref[at : at + depth, :],
                preferred_element_type=jnp.float32,
            )
        for b, (result, place) in enumerate(places):
            out_refs[result][place, :pairs] = (
                base[padded * b : padded * b + rows]
                .astype(jnp.bfloat16)
                .reshape(pairs, 2, columns)
            )
        for k in range(owner_count):
            delta = jnp.dot(
                chosen, u_ref[:, columns * k : columns * (k + 1)], preferred_element_type=jnp.float32
            ).astype(jnp.bfloat16)
            for b, (result, place) in enumerate(places):
                out_refs[result][place, pairs + k] = delta[
                    OWNER_ROW_LIMIT * b : OWNER_ROW_LIMIT * (b + 1)
                ]

    return pl.pallas_call(
        kernel,
        out_shape=[
            jax.ShapeDtypeStruct((2, pairs + owner_count, 2, columns), jnp.bfloat16)
            for _ in range(results)
        ],
        in_specs=[SMEM] + [VMEM] * (count + 4),
        out_specs=[VMEM] * results,
        scratch_shapes=[
            pltpu.VMEM((padded * count, width), jnp.bfloat16),
            pltpu.VMEM((1, padded * count), jnp.int32),
        ],
        compiler_params=pltpu.CompilerParams(vmem_limit_bytes=16 * MIB),
        cost_estimate=pl.CostEstimate(
            flops=2 * padded * count * width * (columns + ranks),
            bytes_accessed=width * (columns + 2 * ranks) * 2,
            transcendentals=0,
        ),
        name="block_products",
    )(sources, row_place, *blocks, base_weight, down, up)


def others(received, before):
    count = len(received)

    def kernel(*refs):
        o_ref, sem = refs[-2], refs[-1]
        copies = [
            pltpu.make_async_copy(refs[i].at[1], o_ref.at[i], sem.at[i]) for i in range(count)
        ]
        for copy in copies:
            copy.start()
        for copy in copies:
            copy.wait()

    return pl.pallas_call(
        kernel,
        out_shape=jax.ShapeDtypeStruct((count,) + received[0].shape[1:], received[0].dtype),
        in_specs=[VMEM] * count + [ANY] * len(before),
        out_specs=VMEM,
        scratch_shapes=[pltpu.SemaphoreType.DMA((count,))],
        compiler_params=pltpu.CompilerParams(vmem_limit_bytes=8 * MIB),
        name="others",
    )(*received, *before)


def assemble(sources, row_place, received, adapters, rows):
    arrays = [array for array, _ in received]
    at_of = [(i, at) for i, (_, ats) in enumerate(received) for at in ats]
    count = len(at_of)
    pairs = rows // 2
    columns = arrays[0].shape[-1]
    slots = OWNER_ROW_LIMIT * count

    def kernel(src_ref, place_ref, *refs):
        me = lax.axis_index("owner")
        o_ref, delta_ref, sem = refs[-3:]
        piece_refs = [refs[i].at[at] for i, at in at_of]
        copies = [
            pltpu.make_async_copy(ref.at[pl.ds(pairs, count)], delta_ref.at[:, a], sem.at[a])
            for a, ref in enumerate(piece_refs)
        ]
        for copy in copies:
            copy.start()
        place = place_ref[pl.ds(me, 1), :]
        owner = place // (adapters * OWNER_ROW_LIMIT)
        place = place % OWNER_ROW_LIMIT
        slot = lax.broadcasted_iota(jnp.int32, (slots, rows), 0)
        piece, second = slot // OWNER_ROW_LIMIT, slot % OWNER_ROW_LIMIT
        match = jnp.zeros((slots, rows), jnp.float32)
        for a in range(count):
            match = jnp.where(
                (piece == a) & (owner == src_ref[me, a]) & (place == second), 1.0, match
            )
        pick = match.T.astype(jnp.bfloat16)
        for copy in copies:
            copy.wait()
        for a, ref in enumerate(piece_refs):
            delta = jnp.dot(
                pick,
                delta_ref[src_ref[me, a]].reshape(slots, columns),
                preferred_element_type=jnp.float32,
            )
            base = ref[:pairs].reshape(rows, columns).astype(jnp.float32)
            span = pl.ds(pl.multiple_of(src_ref[me, a] * columns, columns), columns)
            o_ref[:, span] = (base + adapter_scale * delta).astype(o_ref.dtype)

    return pl.pallas_call(
        kernel,
        out_shape=jax.ShapeDtypeStruct((rows, count * columns), jnp.bfloat16),
        in_specs=[SMEM] + [VMEM] * (len(arrays) + 1),
        out_specs=VMEM,
        scratch_shapes=[
            pltpu.VMEM((count, count, 2, columns), jnp.bfloat16),
            pltpu.SemaphoreType.DMA((count,)),
        ],
        compiler_params=pltpu.CompilerParams(vmem_limit_bytes=16 * MIB),
        name="assemble",
    )(sources, row_place, *arrays)


def per_device(
    states, row_adapter_index, adapter_storage_slot, base_weight, down_weight, up_weight
):
    owner_count = lax.axis_size("owner")
    rows, width = states.shape
    adapters, rank = down_weight.shape[0], down_weight.shape[2]
    turned, swap, sources = ring_tables(owner_count)
    send = functools.partial(lax.ppermute, axis_name="owner")

    down = down_weight.transpose(0, 2, 1).reshape(adapters * rank, width)
    up = up_weight.reshape(adapters * rank, width)

    row_place = row_places(row_adapter_index, adapter_storage_slot, rows, adapters)
    chips = owner_count // 2
    last = chips // 2
    split = [list(range(at - 1, at + 1)) for at in range(last, 2, -2)][::-1]
    split = [list(range(split[0][0] if split else last + 1))] + split
    order, at = [], 0
    for hops in split:
        came = sum(2 if 0 < 2 * hop < chips else 1 for hop in hops)
        order += [at + 2 * i for i in range(came)] + [at + 2 * i + 1 for i in range(came)]
        at += 2 * came
    block_from, piece_from = jnp.asarray(sources[0]), jnp.asarray(sources[1][:, order])

    base_weight, down, up = (
        pltpu.with_memory_space_constraint(w, pltpu.HBM) for w in (base_weight, down, up)
    )
    own = pair_rows(states)
    first, second = own, send(own, perm=swap)
    groups = [[first, second]]
    held = [None] * 3
    received = []

    def products(hops, start):
        blocks, places, result = [], [], 0
        for hop in hops:
            blocks += groups[hop]
            if len(groups[hop]) == 4:
                places += [(result, 0), (result + 1, 1), (result, 1), (result + 1, 0)]
                result += 2
            else:
                places += [(result, 0), (result, 1)]
                result += 1
        out = block_products(
            block_from, start, row_place, blocks, places, held, rank, owner_count
        )
        came, at = [], 0
        for hop in hops:
            came.append(send(out[at], perm=turned(-hop)) if hop else out[at])
            at += 1
            if len(groups[hop]) == 4:
                came.append(send(out[at], perm=turned(hop)))
                at += 1
        received.append(came)
        return len(blocks), out[0]

    done = 0
    for hops in range(1, last + 1):
        first = send(first, perm=turned(1))
        if hops == 1:
            held[0], first = hold(base_weight, first, [row_place])
        if hops == min(2, last):
            held[2], first = hold(up, first, [])
        if hops == last and len(split) > 1:
            for early in split[:-1]:
                count, made = products(early, done)
                done += count
            first = after(first, [made])
        group = [first, send(first, perm=swap)]
        if 2 * hops < chips:
            second = send(second, perm=turned(1))
            if hops == 1:
                held[1], second = hold(down, second, [], turn=True)
            group += [second, send(second, perm=swap)]
        groups.append(group)
    if held[1] is None:
        held[1], row_place = hold(down, row_place, [], turn=True)
    _, made = products(split[-1], done)
    arrays = []
    for came in received:
        passed = send(others(came, [made]), perm=swap)
        arrays += [(array, (0,)) for array in came] + [(passed, tuple(range(len(came))))]
    return assemble(piece_from, row_place, arrays, adapters, rows)


def solution(mesh):
    return jax.shard_map(
        per_device,
        mesh=mesh,
        in_specs=(
            P(("groups", "owner"), None),
            P("groups"),
            P("groups"),
            P(None, "owner"),
            P("owner", None, None),
            P("owner", None, None),
        ),
        out_specs=P(("groups", "owner"), None),
        check_vma=False,
    )
```

```python
import functools

import jax
import jax.numpy as jnp
import numpy as np
from jax import lax
from jax.experimental import pallas as pl
from jax.experimental.pallas import tpu as pltpu
from jax.sharding import PartitionSpec as P

OWNER_ROW_LIMIT = 2
ROW_PAD = 16
adapter_scale = 0.5

VMEM = pl.BlockSpec(memory_space=pltpu.VMEM)
SMEM = pl.BlockSpec(memory_space=pltpu.SMEM)
ANY = pl.BlockSpec(memory_space=pl.ANY)
MIB = 1 << 20


def ring_order(chips):
    return list(range(0, chips, 2)) + list(range(1, chips, 2))[::-1]


def ring_tables(owner_count):
    chips = owner_count // 2
    order = ring_order(chips)
    place = {chip: at for at, chip in enumerate(order)}

    def beside(chip, hops):
        return order[(place[chip] + hops) % chips]

    def turned(hops):
        return [
            (2 * chip + core, 2 * beside(chip, -hops if core else hops) + core)
            for chip in range(chips)
            for core in range(2)
        ]

    swap = [(device, device ^ 1) for device in range(owner_count)]
    sources = np.zeros((2, owner_count, owner_count), np.int32)
    for device in range(owner_count):
        chip, core = divmod(device, 2)
        blocks, pieces = [device, device ^ 1], [[device, device ^ 1]]
        for hops in range(1, chips // 2 + 1):
            mine = 2 * beside(chip, hops if core else -hops)
            mates = 2 * beside(chip, -hops if core else hops)
            if 2 * hops < chips:
                blocks += [mine + core, mates + 1 - core, mine + 1 - core, mates + core]
                pieces += [[mates + core, mine + 1 - core], [mine + core, mates + 1 - core]]
            else:
                blocks += [mine + core, mates + 1 - core]
                pieces += [[mine + core, mine + 1 - core]]
        assert sorted(blocks) == sorted(sum(pieces, [])) == list(range(owner_count))
        sources[0, device], sources[1, device] = blocks, sum(pieces, [])
    return turned, swap, sources


def pair_rows(x):
    rows, width = x.shape

    def kernel(x_ref, o_ref):
        o_ref[...] = x_ref[...].reshape(rows // 2, 2, width)

    return pl.pallas_call(
        kernel,
        out_shape=jax.ShapeDtypeStruct((rows // 2, 2, width), x.dtype),
        in_specs=[VMEM],
        out_specs=VMEM,
        compiler_params=pltpu.CompilerParams(vmem_limit_bytes=4 * MIB),
        name="pair_rows",
    )(x)


def row_places(row_adapter_index, adapter_storage_slot, rows, adapters):
    total, slots = row_adapter_index.shape[0], adapter_storage_slot.shape[0]

    def kernel(index_ref, table_ref, o_ref):
        adapter = lax.broadcasted_iota(jnp.int32, (slots, total), 0)
        slot = jnp.sum(
            jnp.where(adapter == index_ref[...], table_ref[...], 0), axis=0, keepdims=True
        )
        owner = slot // adapters
        at = lax.broadcasted_iota(jnp.int32, (1, total), 1) % rows
        earlier = jnp.zeros_like(slot)
        for back in range(1, rows):
            same = (pltpu.roll(owner, back, 1) == owner) & (at >= back)
            earlier += same.astype(jnp.int32)
        place = slot * OWNER_ROW_LIMIT + earlier
        for group in range(total // rows):
            o_ref[group : group + 1] = place[:, group * rows : (group + 1) * rows]

    return pl.pallas_call(
        kernel,
        out_shape=jax.ShapeDtypeStruct((total // rows, rows), jnp.int32),
        in_specs=[VMEM, VMEM],
        out_specs=VMEM,
        compiler_params=pltpu.CompilerParams(vmem_limit_bytes=8 * MIB),
        name="row_places",
    )(row_adapter_index.reshape(1, total), adapter_storage_slot.reshape(slots, 1))


def hold(weight, carry, before, turn=False):
    shape = weight.shape[::-1] if turn else weight.shape
    parts = 8

    def kernel(*refs):
        src, dst, sem = refs[0], refs[2 + len(before)], refs[-1]
        landing = refs[-2] if turn else dst
        copies = []
        size = weight.shape[1 if turn else 0] // parts
        spans = [pl.ds(part * size, size) for part in range(parts)]
        for part, span in enumerate(spans):
            at = (slice(None), span) if turn else (span,)
            copies.append(pltpu.make_async_copy(src.at[at], landing.at[at], sem.at[part]))
        for copy in copies:
            copy.start()
        for copy, span in zip(copies, spans):
            copy.wait()
            if turn:
                dst[span, :] = landing[:, span].T

    return pl.pallas_call(
        kernel,
        out_shape=[
            pltpu.VMEM(shape, weight.dtype),
            jax.ShapeDtypeStruct(carry.shape, carry.dtype),
        ],
        in_specs=[ANY] * (2 + len(before)),
        out_specs=[VMEM, ANY],
        input_output_aliases={1: 1},
        scratch_shapes=([pltpu.VMEM(weight.shape, weight.dtype)] if turn else [])
        + [pltpu.SemaphoreType.DMA((parts,))],
        compiler_params=pltpu.CompilerParams(vmem_limit_bytes=(8 if turn else 1) * MIB),
        name="hold",
    )(weight, carry, *before)


def after(x, before):
    def kernel(*refs):
        pass

    return pl.pallas_call(
        kernel,
        out_shape=jax.ShapeDtypeStruct(x.shape, x.dtype),
        in_specs=[ANY] * (1 + len(before)),
        out_specs=ANY,
        input_output_aliases={0: 0},
        compiler_params=pltpu.CompilerParams(vmem_limit_bytes=1 * MIB),
        name="after",
    )(x, *before)


def block_products(
    sources, start, row_place, blocks, places, weights, rank, owner_count, before
):
    base_weight, down, up = weights
    count = len(blocks)
    results = 1 + max(result for result, _ in places)
    pairs, _, width = blocks[0].shape
    rows = 2 * pairs
    padded = -(-rows // ROW_PAD) * ROW_PAD
    columns = base_weight.shape[1]
    ranks = down.shape[1]
    depth = min(width, 1024)
    parts = width // depth
    adapters = ranks // rank
    taken = OWNER_ROW_LIMIT * adapters
    takes = -(-OWNER_ROW_LIMIT * count // 8) * 8

    def kernel(src_ref, place_ref, *refs):
        me = lax.axis_index("owner")
        block_refs = refs[:count]
        w_ref, d_ref, u_ref = refs[count : count + 3]
        out_refs = refs[count + 3 + len(before) :][:results]
        x_ref, code_ref = refs[-2:]
        for b in range(count):
            x_ref[padded * b : padded * b + rows] = block_refs[b][...].reshape(rows, width)
            x_ref[padded * b + rows : padded * (b + 1)] = jnp.zeros(
                (padded - rows, width), x_ref.dtype
            )
        low = jnp.zeros((padded * count, ranks), jnp.float32)
        for part in range(parts):
            at = part * depth
            low += jnp.dot(
                x_ref[:, at : at + depth],
                d_ref[at : at + depth, :],
                preferred_element_type=jnp.float32,
            )
        low = low.astype(jnp.bfloat16)
        base = jnp.zeros((padded * count, columns), jnp.float32)
        for part in range(parts):
            at = part * depth
            base += jnp.dot(
                x_ref[:, at : at + depth],
                w_ref[at : at + depth, :],
                preferred_element_type=jnp.float32,
            )
        code_ref[...] = jnp.full_like(code_ref, -1)
        for b in range(count):
            code_ref[:, padded * b : padded * b + rows] = (
                place_ref[pl.ds(src_ref[me, start + b], 1), :] - me * taken
            )
        row = lax.broadcasted_iota(jnp.int32, (adapters * takes, padded * count), 0)
        lane = lax.broadcasted_iota(jnp.int32, (adapters * takes, padded * count), 1)
        place = row % takes
        wanted = row // takes * OWNER_ROW_LIMIT + place % OWNER_ROW_LIMIT
        match = (code_ref[...] == wanted) & (lane // padded == place // OWNER_ROW_LIMIT)
        found = jnp.dot(match.astype(jnp.bfloat16), low, preferred_element_type=jnp.float32)
        adapter = lax.broadcasted_iota(jnp.int32, (takes, ranks), 1) // rank
        chosen = jnp.zeros((takes, ranks), jnp.float32)
        for a in range(adapters):
            chosen = jnp.where(adapter == a, found[takes * a : takes * (a + 1)], chosen)
        chosen = chosen.astype(jnp.bfloat16)
        for b, (result, place) in enumerate(places):
            out_refs[result][place, :pairs] = (
                base[padded * b : padded * b + rows]
                .astype(jnp.bfloat16)
                .reshape(pairs, 2, columns)
            )
        for k in range(owner_count):
            delta = jnp.dot(
                chosen, u_ref[:, columns * k : columns * (k + 1)], preferred_element_type=jnp.float32
            ).astype(jnp.bfloat16)
            for b, (result, place) in enumerate(places):
                out_refs[result][place, pairs + k] = delta[
                    OWNER_ROW_LIMIT * b : OWNER_ROW_LIMIT * (b + 1)
                ]

    return pl.pallas_call(
        kernel,
        out_shape=[
            jax.ShapeDtypeStruct((2, pairs + owner_count, 2, columns), jnp.bfloat16)
            for _ in range(results)
        ],
        in_specs=[SMEM] + [VMEM] * (count + 4) + [ANY] * len(before),
        out_specs=[VMEM] * results,
        scratch_shapes=[
            pltpu.VMEM((padded * count, width), jnp.bfloat16),
            pltpu.VMEM((1, padded * count), jnp.int32),
        ],
        compiler_params=pltpu.CompilerParams(vmem_limit_bytes=16 * MIB),
        cost_estimate=pl.CostEstimate(
            flops=2 * padded * count * width * (columns + ranks),
            bytes_accessed=width * (columns + 2 * ranks) * 2,
            transcendentals=0,
        ),
        name="block_products",
    )(sources, row_place, *blocks, base_weight, down, up, *before)


def others(received, before):
    count = len(received)

    def kernel(*refs):
        o_ref, sem = refs[-2], refs[-1]
        copies = [
            pltpu.make_async_copy(refs[i].at[1], o_ref.at[i], sem.at[i]) for i in range(count)
        ]
        for copy in copies:
            copy.start()
        for copy in copies:
            copy.wait()

    return pl.pallas_call(
        kernel,
        out_shape=jax.ShapeDtypeStruct((count,) + received[0].shape[1:], received[0].dtype),
        in_specs=[VMEM] * count + [ANY] * len(before),
        out_specs=VMEM,
        scratch_shapes=[pltpu.SemaphoreType.DMA((count,))],
        compiler_params=pltpu.CompilerParams(vmem_limit_bytes=8 * MIB),
        name="others",
    )(*received, *before)


def assemble(sources, row_place, received, adapters, rows):
    arrays = [array for array, _ in received]
    at_of = [(i, at) for i, (_, ats) in enumerate(received) for at in ats]
    count = len(at_of)
    pairs = rows // 2
    columns = arrays[0].shape[-1]
    slots = OWNER_ROW_LIMIT * count

    def kernel(src_ref, place_ref, *refs):
        me = lax.axis_index("owner")
        o_ref, delta_ref, sem = refs[-3:]
        piece_refs = [refs[i].at[at] for i, at in at_of]
        copies = [
            pltpu.make_async_copy(ref.at[pl.ds(pairs, count)], delta_ref.at[:, a], sem.at[a])
            for a, ref in enumerate(piece_refs)
        ]
        for copy in copies:
            copy.start()
        place = place_ref[pl.ds(me, 1), :]
        owner = place // (adapters * OWNER_ROW_LIMIT)
        place = place % OWNER_ROW_LIMIT
        slot = lax.broadcasted_iota(jnp.int32, (slots, rows), 0)
        piece, second = slot // OWNER_ROW_LIMIT, slot % OWNER_ROW_LIMIT
        match = jnp.zeros((slots, rows), jnp.float32)
        for a in range(count):
            match = jnp.where(
                (piece == a) & (owner == src_ref[me, a]) & (place == second), 1.0, match
            )
        pick = match.T.astype(jnp.bfloat16)
        for copy in copies:
            copy.wait()
        for a, ref in enumerate(piece_refs):
            delta = jnp.dot(
                pick,
                delta_ref[src_ref[me, a]].reshape(slots, columns),
                preferred_element_type=jnp.float32,
            )
            base = ref[:pairs].reshape(rows, columns).astype(jnp.float32)
            span = pl.ds(pl.multiple_of(src_ref[me, a] * columns, columns), columns)
            o_ref[:, span] = (base + adapter_scale * delta).astype(o_ref.dtype)

    return pl.pallas_call(
        kernel,
        out_shape=jax.ShapeDtypeStruct((rows, count * columns), jnp.bfloat16),
        in_specs=[SMEM] + [VMEM] * (len(arrays) + 1),
        out_specs=VMEM,
        scratch_shapes=[
            pltpu.VMEM((count, count, 2, columns), jnp.bfloat16),
            pltpu.SemaphoreType.DMA((count,)),
        ],
        compiler_params=pltpu.CompilerParams(vmem_limit_bytes=16 * MIB),
        name="assemble",
    )(sources, row_place, *arrays)


def per_device(
    states, row_adapter_index, adapter_storage_slot, base_weight, down_weight, up_weight
):
    owner_count = lax.axis_size("owner")
    rows, width = states.shape
    adapters, rank = down_weight.shape[0], down_weight.shape[2]
    turned, swap, sources = ring_tables(owner_count)
    send = functools.partial(lax.ppermute, axis_name="owner")

    down = down_weight.transpose(0, 2, 1).reshape(adapters * rank, width)
    up = up_weight.reshape(adapters * rank, width)

    row_place = row_places(row_adapter_index, adapter_storage_slot, rows, adapters)
    chips = owner_count // 2
    last = chips // 2
    split = [list(range(at - 1, at + 1)) for at in range(last, 2, -2)][::-1]
    split = [list(range(split[0][0] if split else last + 1))] + split
    order, at = [], 0
    for hops in split:
        came = sum(2 if 0 < 2 * hop < chips else 1 for hop in hops)
        order += [at + 2 * i for i in range(came)] + [at + 2 * i + 1 for i in range(came)]
        at += 2 * came
    block_from, piece_from = jnp.asarray(sources[0]), jnp.asarray(sources[1][:, order])

    base_weight, down, up = (
        pltpu.with_memory_space_constraint(w, pltpu.HBM) for w in (base_weight, down, up)
    )
    own = pair_rows(states)
    first, second = own, send(own, perm=swap)
    groups = [[first, second]]
    held = [None] * 3
    received = []

    def products(hops, start, before):
        blocks, places, result = [], [], 0
        for hop in hops:
            blocks += groups[hop]
            if len(groups[hop]) == 4:
                places += [(result, 0), (result + 1, 1), (result, 1), (result + 1, 0)]
                result += 2
            else:
                places += [(result, 0), (result, 1)]
                result += 1
        out = block_products(
            block_from, start, row_place, blocks, places, held, rank, owner_count, before
        )
        came, at = [], 0
        for hop in hops:
            came.append(send(out[at], perm=turned(-hop)) if hop else out[at])
            at += 1
            if len(groups[hop]) == 4:
                came.append(send(out[at], perm=turned(hop)))
                at += 1
        received.append(came)
        return len(blocks), out[0]

    done = 0
    for hops in range(1, last + 1):
        first = send(first, perm=turned(1))
        if hops == 1:
            held[0], first = hold(base_weight, first, [row_place])
        if hops == min(2, last):
            held[2], first = hold(up, first, [])
        if hops == last and len(split) > 1:
            for early in split[:-1]:
                count, made = products(early, done, [second])
                done += count
            first = after(first, [made])
        group = [first, send(first, perm=swap)]
        if 2 * hops < chips:
            second = send(second, perm=turned(1))
            if hops == 1:
                held[1], second = hold(down, second, [], turn=True)
            group += [second, send(second, perm=swap)]
        groups.append(group)
    if held[1] is None:
        held[1], row_place = hold(down, row_place, [], turn=True)
    _, made = products(split[-1], done, [])
    arrays = []
    for came in received:
        passed = send(others(came, [made]), perm=swap)
        arrays += [(array, (0,)) for array in came] + [(passed, tuple(range(len(came))))]
    return assemble(piece_from, row_place, arrays, adapters, rows)


def solution(mesh):
    return jax.shard_map(
        per_device,
        mesh=mesh,
        in_specs=(
            P(("groups", "owner"), None),
            P("groups"),
            P("groups"),
            P(None, "owner"),
            P("owner", None, None),
            P("owner", None, None),
        ),
        out_specs=P(("groups", "owner"), None),
        check_vma=False,
    )
```

```python
import functools

import jax
import jax.numpy as jnp
from jax import lax
from jax.experimental import pallas as pl
from jax.experimental.pallas import tpu as pltpu
from jax.sharding import PartitionSpec as P

OWNER_ROW_LIMIT = 2
ROW_PAD = 16
adapter_scale = 0.5

VMEM = pl.BlockSpec(memory_space=pltpu.VMEM)
ANY = pl.BlockSpec(memory_space=pl.ANY)
MIB = 1 << 20


def on_ring(chips, at):
    at = at % chips
    out = 2 * at < chips
    back = 2 * (chips - 1 - at) + 1
    return jnp.where(out, 2 * at, back) if isinstance(at, jax.Array) else (2 * at if out else back)


def ring_place(chips, chip):
    back = chips - 1 - chip // 2
    if isinstance(chip, jax.Array):
        return jnp.where(chip % 2 == 0, chip // 2, back)
    return back if chip % 2 else chip // 2


def device_of(chips, me, what):
    hops, same = what
    chip, core = me // 2, me % 2
    place = ring_place(chips, chip) + hops * (2 * core - 1)
    return 2 * on_ring(chips, place + chips) + (core if same else 1 - core)


def ring_tables(owner_count):
    chips = owner_count // 2
    devices = range(owner_count)

    def turned(hops):
        return [(device, device_of(chips, device, (-hops, True))) for device in devices]

    swap = [(device, device ^ 1) for device in devices]
    blocks, pieces = [(0, True), (0, False)], [(0, True), (0, False)]
    for hops in range(1, chips // 2 + 1):
        if 2 * hops < chips:
            blocks += [(hops, True), (-hops, False), (hops, False), (-hops, True)]
            pieces += [(-hops, True), (hops, False), (hops, True), (-hops, False)]
        else:
            blocks += [(hops, True), (-hops, False)]
            pieces += [(hops, True), (hops, False)]
    for device in devices:
        for what in (blocks, pieces):
            assert sorted(device_of(chips, device, w) for w in what) == list(devices)
    return turned, swap, blocks, pieces


def pair_rows(x):
    rows, width = x.shape

    def kernel(x_ref, o_ref):
        o_ref[...] = x_ref[...].reshape(rows // 2, 2, width)

    return pl.pallas_call(
        kernel,
        out_shape=jax.ShapeDtypeStruct((rows // 2, 2, width), x.dtype),
        in_specs=[VMEM],
        out_specs=VMEM,
        compiler_params=pltpu.CompilerParams(vmem_limit_bytes=4 * MIB),
        name="pair_rows",
    )(x)


def row_places(row_adapter_index, adapter_storage_slot, rows, adapters):
    total, slots = row_adapter_index.shape[0], adapter_storage_slot.shape[0]

    def kernel(index_ref, table_ref, o_ref):
        adapter = lax.broadcasted_iota(jnp.int32, (slots, total), 0)
        slot = jnp.sum(
            jnp.where(adapter == index_ref[...], table_ref[...], 0), axis=0, keepdims=True
        )
        owner = slot // adapters
        at = lax.broadcasted_iota(jnp.int32, (1, total), 1) % rows
        earlier = jnp.zeros_like(slot)
        for back in range(1, rows):
            same = (pltpu.roll(owner, back, 1) == owner) & (at >= back)
            earlier += same.astype(jnp.int32)
        place = slot * OWNER_ROW_LIMIT + earlier
        for group in range(total // rows):
            o_ref[group : group + 1] = place[:, group * rows : (group + 1) * rows]

    return pl.pallas_call(
        kernel,
        out_shape=jax.ShapeDtypeStruct((total // rows, rows), jnp.int32),
        in_specs=[VMEM, VMEM],
        out_specs=VMEM,
        compiler_params=pltpu.CompilerParams(vmem_limit_bytes=8 * MIB),
        name="row_places",
    )(row_adapter_index.reshape(1, total), adapter_storage_slot.reshape(slots, 1))


def hold(weight, carry, before, turn=False, half=None):
    shape = weight.shape[::-1] if turn else weight.shape
    if half is not None:
        shape = (shape[0] // 2, shape[1])
    parts = 8

    def kernel(*refs):
        src, dst, sem = refs[0], refs[2 + len(before)], refs[-1]
        landing = refs[-2] if turn else dst
        copies = []
        size = shape[0] // parts
        spans = [pl.ds(part * size, size) for part in range(parts)]
        for part, span in enumerate(spans):
            at = (slice(None), span) if turn else (span,)
            of = (pl.ds(half * shape[0] + part * size, size),) if half else at
            copies.append(pltpu.make_async_copy(src.at[of], landing.at[at], sem.at[part]))
        for copy in copies:
            copy.start()
        for copy, span in zip(copies, spans):
            copy.wait()
            if turn:
                dst[span, :] = landing[:, span].T

    return pl.pallas_call(
        kernel,
        out_shape=[
            pltpu.VMEM(shape, weight.dtype),
            jax.ShapeDtypeStruct(carry.shape, carry.dtype),
        ],
        in_specs=[ANY] * (2 + len(before)),
        out_specs=[VMEM, ANY],
        input_output_aliases={1: 1},
        scratch_shapes=([pltpu.VMEM(weight.shape, weight.dtype)] if turn else [])
        + [pltpu.SemaphoreType.DMA((parts,))],
        compiler_params=pltpu.CompilerParams(vmem_limit_bytes=(8 if turn else 1) * MIB),
        name="hold",
    )(weight, carry, *before)


def after(x, before):
    def kernel(*refs):
        pass

    return pl.pallas_call(
        kernel,
        out_shape=jax.ShapeDtypeStruct(x.shape, x.dtype),
        in_specs=[ANY] * (1 + len(before)),
        out_specs=ANY,
        input_output_aliases={0: 0},
        compiler_params=pltpu.CompilerParams(vmem_limit_bytes=1 * MIB),
        name="after",
    )(x, *before)


def block_products(
    sources, row_place, blocks, places, weights, rank, owner_count, before
):
    base_low, base_high, down, up = weights
    count = len(blocks)
    results = 1 + max(result for result, _ in places)
    pairs, _, width = blocks[0].shape
    rows = 2 * pairs
    padded = -(-rows // ROW_PAD) * ROW_PAD
    columns = base_low.shape[1]
    ranks = down.shape[1]
    depth = min(width // 2, 1024)
    parts = width // depth
    adapters = ranks // rank
    taken = OWNER_ROW_LIMIT * adapters
    takes = -(-OWNER_ROW_LIMIT * count // 8) * 8

    def kernel(place_ref, *refs):
        me = lax.axis_index("owner")
        block_refs = refs[:count]
        *w_refs, d_ref, u_ref = refs[count : count + 4]
        out_refs = refs[count + 4 + len(before) :][:results]
        x_ref, code_ref = refs[-2:]
        for b in range(count):
            x_ref[padded * b : padded * b + rows] = block_refs[b][...].reshape(rows, width)
            x_ref[padded * b + rows : padded * (b + 1)] = jnp.zeros(
                (padded - rows, width), x_ref.dtype
            )
        low = jnp.zeros((padded * count, ranks), jnp.float32)
        for part in range(parts):
            at = part * depth
            low += jnp.dot(
                x_ref[:, at : at + depth],
                d_ref[at : at + depth, :],
                preferred_element_type=jnp.float32,
            )
        low = low.astype(jnp.bfloat16)
        base = jnp.zeros((padded * count, columns), jnp.float32)
        for part in range(parts):
            at = part * depth
            base += jnp.dot(
                x_ref[:, at : at + depth],
                w_refs[2 * part // parts][at % (width // 2) : at % (width // 2) + depth, :],
                preferred_element_type=jnp.float32,
            )
        code_ref[...] = jnp.full_like(code_ref, -1)
        for b in range(count):
            code_ref[:, padded * b : padded * b + rows] = (
                place_ref[pl.ds(device_of(owner_count // 2, me, sources[b]), 1), :] - me * taken
            )
        row = lax.broadcasted_iota(jnp.int32, (adapters * takes, padded * count), 0)
        lane = lax.broadcasted_iota(jnp.int32, (adapters * takes, padded * count), 1)
        place = row % takes
        wanted = row // takes * OWNER_ROW_LIMIT + place % OWNER_ROW_LIMIT
        match = (code_ref[...] == wanted) & (lane // padded == place // OWNER_ROW_LIMIT)
        found = jnp.dot(match.astype(jnp.bfloat16), low, preferred_element_type=jnp.float32)
        adapter = lax.broadcasted_iota(jnp.int32, (takes, ranks), 1) // rank
        chosen = jnp.zeros((takes, ranks), jnp.float32)
        for a in range(adapters):
            chosen = jnp.where(adapter == a, found[takes * a : takes * (a + 1)], chosen)
        chosen = chosen.astype(jnp.bfloat16)
        for b, (result, place) in enumerate(places):
            out_refs[result][place, :pairs] = (
                base[padded * b : padded * b + rows]
                .astype(jnp.bfloat16)
                .reshape(pairs, 2, columns)
            )
        for k in range(owner_count):
            delta = jnp.dot(
                chosen, u_ref[:, columns * k : columns * (k + 1)], preferred_element_type=jnp.float32
            ).astype(jnp.bfloat16)
            for b, (result, place) in enumerate(places):
                out_refs[result][place, pairs + k] = delta[
                    OWNER_ROW_LIMIT * b : OWNER_ROW_LIMIT * (b + 1)
                ]

    return pl.pallas_call(
        kernel,
        out_shape=[
            jax.ShapeDtypeStruct((2, pairs + owner_count, 2, columns), jnp.bfloat16)
            for _ in range(results)
        ],
        in_specs=[VMEM] * (count + 5) + [ANY] * len(before),
        out_specs=[VMEM] * results,
        scratch_shapes=[
            pltpu.VMEM((padded * count, width), jnp.bfloat16),
            pltpu.VMEM((1, padded * count), jnp.int32),
        ],
        compiler_params=pltpu.CompilerParams(vmem_limit_bytes=16 * MIB),
        cost_estimate=pl.CostEstimate(
            flops=2 * padded * count * width * (columns + ranks),
            bytes_accessed=width * (columns + 2 * ranks) * 2,
            transcendentals=0,
        ),
        name="block_products",
    )(row_place, *blocks, base_low, base_high, down, up, *before)


def others(received, before):
    count = len(received)

    def kernel(*refs):
        o_ref, sem = refs[-2], refs[-1]
        copies = [
            pltpu.make_async_copy(refs[i].at[1], o_ref.at[i], sem.at[i]) for i in range(count)
        ]
        for copy in copies:
            copy.start()
        for copy in copies:
            copy.wait()

    return pl.pallas_call(
        kernel,
        out_shape=jax.ShapeDtypeStruct((count,) + received[0].shape[1:], received[0].dtype),
        in_specs=[VMEM] * count + [ANY] * len(before),
        out_specs=VMEM,
        scratch_shapes=[pltpu.SemaphoreType.DMA((count,))],
        compiler_params=pltpu.CompilerParams(vmem_limit_bytes=8 * MIB),
        name="others",
    )(*received, *before)


def assemble(sources, row_place, received, adapters, rows):
    arrays = [array for array, _ in received]
    at_of = [(i, at) for i, (_, ats) in enumerate(received) for at in ats]
    count = len(at_of)
    pairs = rows // 2
    columns = arrays[0].shape[-1]
    slots = OWNER_ROW_LIMIT * count

    def kernel(place_ref, *refs):
        me = lax.axis_index("owner")
        source = [device_of(count // 2, me, what) for what in sources]
        o_ref, delta_ref, row_ref, out_sem = refs[-4:]
        piece_refs = [refs[i].at[at] for i, at in at_of]
        for a, ref in enumerate(piece_refs):
            delta_ref[:, a] = ref[pairs:]
        place = place_ref[pl.ds(me, 1), :]
        owner = place // (adapters * OWNER_ROW_LIMIT)
        place = place % OWNER_ROW_LIMIT
        slot = lax.broadcasted_iota(jnp.int32, (slots, rows), 0)
        piece, second = slot // OWNER_ROW_LIMIT, slot % OWNER_ROW_LIMIT
        match = jnp.zeros((slots, rows), jnp.float32)
        for a in range(count):
            match = jnp.where(
                (piece == a) & (owner == source[a]) & (place == second), 1.0, match
            )
        pick = match.T.astype(jnp.bfloat16)
        outs = []
        for a, ref in enumerate(piece_refs):
            delta = jnp.dot(
                pick,
                delta_ref[source[a]].reshape(slots, columns),
                preferred_element_type=jnp.float32,
            )
            base = ref[:pairs].reshape(rows, columns).astype(jnp.float32)
            row_ref[a] = (base + adapter_scale * delta).astype(row_ref.dtype)
            span = pl.ds(pl.multiple_of(source[a] * columns, columns), columns)
            outs.append(pltpu.make_async_copy(row_ref.at[a], o_ref.at[:, span], out_sem.at[a]))
            outs[-1].start()
        for copy in outs:
            copy.wait()

    return pl.pallas_call(
        kernel,
        out_shape=jax.ShapeDtypeStruct((rows, count * columns), jnp.bfloat16),
        in_specs=[VMEM] * (len(arrays) + 1),
        out_specs=ANY,
        scratch_shapes=[
            pltpu.VMEM((count, count, 2, columns), jnp.bfloat16),
            pltpu.VMEM((count, rows, columns), jnp.bfloat16),
            pltpu.SemaphoreType.DMA((count,)),
        ],
        compiler_params=pltpu.CompilerParams(vmem_limit_bytes=16 * MIB),
        name="assemble",
    )(row_place, *arrays)


def per_device(
    states, row_adapter_index, adapter_storage_slot, base_weight, down_weight, up_weight
):
    owner_count = lax.axis_size("owner")
    rows, width = states.shape
    adapters, rank = down_weight.shape[0], down_weight.shape[2]
    turned, swap, block_from, piece_from = ring_tables(owner_count)
    send = functools.partial(lax.ppermute, axis_name="owner")

    down = down_weight.transpose(0, 2, 1).reshape(adapters * rank, width)
    up = up_weight.reshape(adapters * rank, width)

    row_place = row_places(row_adapter_index, adapter_storage_slot, rows, adapters)
    chips = owner_count // 2
    last = chips // 2
    split = [list(range(at - 1, at + 1)) for at in range(last, 2, -2)][::-1]
    split = [list(range(split[0][0] if split else last + 1))] + split
    order, at = [], 0
    for hops in split:
        came = sum(2 if 0 < 2 * hop < chips else 1 for hop in hops)
        order += [at + 2 * i for i in range(came)] + [at + 2 * i + 1 for i in range(came)]
        at += 2 * came
    piece_from = [piece_from[i] for i in order]

    base_weight, down, up = (
        pltpu.with_memory_space_constraint(w, pltpu.HBM) for w in (base_weight, down, up)
    )
    own = pair_rows(states)
    first, second = own, send(own, perm=swap)
    groups = [[first, second]]
    held = [None] * 4
    received = []

    def products(hops, start, before):
        blocks, places, result = [], [], 0
        for hop in hops:
            blocks += groups[hop]
            if len(groups[hop]) == 4:
                places += [(result, 0), (result + 1, 1), (result, 1), (result + 1, 0)]
                result += 2
            else:
                places += [(result, 0), (result, 1)]
                result += 1
        out = block_products(
            block_from[start : start + len(blocks)],
            row_place,
            blocks,
            places,
            held,
            rank,
            owner_count,
            before,
        )
        came, at = [], 0
        for hop in hops:
            came.append(send(out[at], perm=turned(-hop)) if hop else out[at])
            at += 1
            if len(groups[hop]) == 4:
                came.append(send(out[at], perm=turned(hop)))
                at += 1
        received.append(came)
        return len(blocks), out[0]

    done = 0
    for hops in range(1, last + 1):
        first = send(first, perm=turned(1))
        if hops == 1:
            held[0], first = hold(base_weight, first, [row_place], half=0)
        if hops == 2:
            held[3], first = hold(up, first, [])
        if hops == last and len(split) > 1:
            for early in split[:-1]:
                count, made = products(early, done, [second])
                done += count
            first = after(first, [made])
        group = [first, send(first, perm=swap)]
        if 2 * hops < chips:
            second = send(second, perm=turned(1))
            if hops == 1:
                held[1], second = hold(base_weight, second, [], half=1)
            if hops == 2:
                held[2], second = hold(down, second, [], turn=True)
            group += [second, send(second, perm=swap)]
        groups.append(group)
    for i, (weight, how) in enumerate(
        [(base_weight, dict(half=0)), (base_weight, dict(half=1)), (down, dict(turn=True)), (up, {})]
    ):
        if held[i] is None:
            held[i], row_place = hold(weight, row_place, [], **how)
    _, made = products(split[-1], done, [])
    arrays = []
    for came in received:
        passed = send(others(came, [made]), perm=swap)
        arrays += [(array, (0,)) for array in came] + [(passed, tuple(range(len(came))))]
    return assemble(piece_from, row_place, arrays, adapters, rows)


def solution(mesh):
    return jax.shard_map(
        per_device,
        mesh=mesh,
        in_specs=(
            P(("groups", "owner"), None),
            P("groups"),
            P("groups"),
            P(None, "owner"),
            P("owner", None, None),
            P("owner", None, None),
        ),
        out_specs=P(("groups", "owner"), None),
        check_vma=False,
    )
```

```python
import functools

import jax
import jax.numpy as jnp
from jax import lax
from jax.experimental import pallas as pl
from jax.experimental.pallas import tpu as pltpu
from jax.sharding import PartitionSpec as P

OWNER_ROW_LIMIT = 2
ROW_PAD = 16
adapter_scale = 0.5

VMEM = pl.BlockSpec(memory_space=pltpu.VMEM)
ANY = pl.BlockSpec(memory_space=pl.ANY)
MIB = 1 << 20


def on_ring(chips, at):
    at = at % chips
    out = 2 * at < chips
    back = 2 * (chips - 1 - at) + 1
    return jnp.where(out, 2 * at, back) if isinstance(at, jax.Array) else (2 * at if out else back)


def ring_place(chips, chip):
    back = chips - 1 - chip // 2
    if isinstance(chip, jax.Array):
        return jnp.where(chip % 2 == 0, chip // 2, back)
    return back if chip % 2 else chip // 2


def device_of(chips, me, what):
    hops, same = what
    chip, core = me // 2, me % 2
    place = ring_place(chips, chip) + hops * (2 * core - 1)
    return 2 * on_ring(chips, place + chips) + (core if same else 1 - core)


def ring_tables(owner_count):
    chips = owner_count // 2
    devices = range(owner_count)

    def turned(hops):
        return [(device, device_of(chips, device, (-hops, True))) for device in devices]

    swap = [(device, device ^ 1) for device in devices]
    blocks, pieces = [(0, True), (0, False)], [(0, True), (0, False)]
    for hops in range(1, chips // 2 + 1):
        if 2 * hops < chips:
            blocks += [(hops, True), (-hops, False), (hops, False), (-hops, True)]
            pieces += [(-hops, True), (hops, False), (hops, True), (-hops, False)]
        else:
            blocks += [(hops, True), (-hops, False)]
            pieces += [(hops, True), (hops, False)]
    for device in devices:
        for what in (blocks, pieces):
            assert sorted(device_of(chips, device, w) for w in what) == list(devices)
    return turned, swap, blocks, pieces


def pair_rows(x):
    rows, width = x.shape

    def kernel(x_ref, o_ref):
        o_ref[...] = x_ref[...].reshape(rows // 2, 2, width)

    return pl.pallas_call(
        kernel,
        out_shape=jax.ShapeDtypeStruct((rows // 2, 2, width), x.dtype),
        in_specs=[VMEM],
        out_specs=VMEM,
        compiler_params=pltpu.CompilerParams(vmem_limit_bytes=4 * MIB),
        name="pair_rows",
    )(x)


def row_places(row_adapter_index, adapter_storage_slot, rows, adapters):
    total, slots = row_adapter_index.shape[0], adapter_storage_slot.shape[0]

    def kernel(index_ref, table_ref, o_ref):
        adapter = lax.broadcasted_iota(jnp.int32, (slots, total), 0)
        slot = jnp.sum(
            jnp.where(adapter == index_ref[...], table_ref[...], 0), axis=0, keepdims=True
        )
        owner = slot // adapters
        at = lax.broadcasted_iota(jnp.int32, (1, total), 1) % rows
        earlier = jnp.zeros_like(slot)
        for back in range(1, rows):
            same = (pltpu.roll(owner, back, 1) == owner) & (at >= back)
            earlier += same.astype(jnp.int32)
        place = slot * OWNER_ROW_LIMIT + earlier
        for group in range(total // rows):
            o_ref[group : group + 1] = place[:, group * rows : (group + 1) * rows]

    return pl.pallas_call(
        kernel,
        out_shape=jax.ShapeDtypeStruct((total // rows, rows), jnp.int32),
        in_specs=[VMEM, VMEM],
        out_specs=VMEM,
        compiler_params=pltpu.CompilerParams(vmem_limit_bytes=8 * MIB),
        name="row_places",
    )(row_adapter_index.reshape(1, total), adapter_storage_slot.reshape(slots, 1))


def hold(weight, carry, before, turn=False, half=None):
    shape = weight.shape[::-1] if turn else weight.shape
    if half is not None:
        shape = (shape[0] // 2, shape[1])
    parts = 8

    def kernel(*refs):
        src, dst, sem = refs[0], refs[2 + len(before)], refs[-1]
        landing = refs[-2] if turn else dst
        copies = []
        size = shape[0] // parts
        spans = [pl.ds(part * size, size) for part in range(parts)]
        for part, span in enumerate(spans):
            at = (slice(None), span) if turn else (span,)
            of = (pl.ds(half * shape[0] + part * size, size),) if half else at
            copies.append(pltpu.make_async_copy(src.at[of], landing.at[at], sem.at[part]))
        for copy in copies:
            copy.start()
        for copy, span in zip(copies, spans):
            copy.wait()
            if turn:
                dst[span, :] = landing[:, span].T

    return pl.pallas_call(
        kernel,
        out_shape=[
            pltpu.VMEM(shape, weight.dtype),
            jax.ShapeDtypeStruct(carry.shape, carry.dtype),
        ],
        in_specs=[ANY] * (2 + len(before)),
        out_specs=[VMEM, ANY],
        input_output_aliases={1: 1},
        scratch_shapes=([pltpu.VMEM(weight.shape, weight.dtype)] if turn else [])
        + [pltpu.SemaphoreType.DMA((parts,))],
        compiler_params=pltpu.CompilerParams(vmem_limit_bytes=(8 if turn else 1) * MIB),
        name="hold",
    )(weight, carry, *before)


def after(x, before):
    def kernel(*refs):
        pass

    return pl.pallas_call(
        kernel,
        out_shape=jax.ShapeDtypeStruct(x.shape, x.dtype),
        in_specs=[ANY] * (1 + len(before)),
        out_specs=ANY,
        input_output_aliases={0: 0},
        compiler_params=pltpu.CompilerParams(vmem_limit_bytes=1 * MIB),
        name="after",
    )(x, *before)


def block_products(
    sources, row_place, blocks, places, weights, rank, owner_count, before
):
    base_low, base_high, down, up = weights
    count = len(blocks)
    results = 1 + max(result for result, _ in places)
    pairs, _, width = blocks[0].shape
    rows = 2 * pairs
    padded = -(-rows // ROW_PAD) * ROW_PAD
    columns = base_low.shape[1]
    ranks = down.shape[1]
    depth = min(width // 2, 1024)
    parts = width // depth
    adapters = ranks // rank
    taken = OWNER_ROW_LIMIT * adapters
    takes = -(-OWNER_ROW_LIMIT * count // 8) * 8

    def kernel(place_ref, *refs):
        me = lax.axis_index("owner")
        block_refs = refs[:count]
        *w_refs, d_ref, u_ref = refs[count : count + 4]
        out_refs = refs[count + 4 + len(before) :][:results]
        x_ref, code_ref = refs[-2:]
        for b in range(count):
            x_ref[padded * b : padded * b + rows] = block_refs[b][...].reshape(rows, width)
            x_ref[padded * b + rows : padded * (b + 1)] = jnp.zeros(
                (padded - rows, width), x_ref.dtype
            )
        low = jnp.zeros((padded * count, ranks), jnp.float32)
        for part in range(parts):
            at = part * depth
            low += jnp.dot(
                x_ref[:, at : at + depth],
                d_ref[at : at + depth, :],
                preferred_element_type=jnp.float32,
            )
        low = low.astype(jnp.bfloat16)
        base = jnp.zeros((padded * count, columns), jnp.float32)
        for part in range(parts):
            at = part * depth
            base += jnp.dot(
                x_ref[:, at : at + depth],
                w_refs[2 * part // parts][at % (width // 2) : at % (width // 2) + depth, :],
                preferred_element_type=jnp.float32,
            )
        code_ref[...] = jnp.full_like(code_ref, -1)
        for b in range(count):
            code_ref[:, padded * b : padded * b + rows] = (
                place_ref[pl.ds(device_of(owner_count // 2, me, sources[b]), 1), :] - me * taken
            )
        row = lax.broadcasted_iota(jnp.int32, (adapters * takes, padded * count), 0)
        lane = lax.broadcasted_iota(jnp.int32, (adapters * takes, padded * count), 1)
        place = row % takes
        wanted = row // takes * OWNER_ROW_LIMIT + place % OWNER_ROW_LIMIT
        match = (code_ref[...] == wanted) & (lane // padded == place // OWNER_ROW_LIMIT)
        found = jnp.dot(match.astype(jnp.bfloat16), low, preferred_element_type=jnp.float32)
        adapter = lax.broadcasted_iota(jnp.int32, (takes, ranks), 1) // rank
        chosen = jnp.zeros((takes, ranks), jnp.float32)
        for a in range(adapters):
            chosen = jnp.where(adapter == a, found[takes * a : takes * (a + 1)], chosen)
        chosen = chosen.astype(jnp.bfloat16)
        for b, (result, place) in enumerate(places):
            out_refs[result][place, :pairs] = (
                base[padded * b : padded * b + rows]
                .astype(jnp.bfloat16)
                .reshape(pairs, 2, columns)
            )
        for k in range(owner_count):
            delta = jnp.dot(
                chosen, u_ref[:, columns * k : columns * (k + 1)], preferred_element_type=jnp.float32
            ).astype(jnp.bfloat16)
            for b, (result, place) in enumerate(places):
                out_refs[result][place, pairs + k] = delta[
                    OWNER_ROW_LIMIT * b : OWNER_ROW_LIMIT * (b + 1)
                ]

    return pl.pallas_call(
        kernel,
        out_shape=[
            jax.ShapeDtypeStruct((2, pairs + owner_count, 2, columns), jnp.bfloat16)
            for _ in range(results)
        ],
        in_specs=[VMEM] * (count + 5) + [ANY] * len(before),
        out_specs=[VMEM] * results,
        scratch_shapes=[
            pltpu.VMEM((padded * count, width), jnp.bfloat16),
            pltpu.VMEM((1, padded * count), jnp.int32),
        ],
        compiler_params=pltpu.CompilerParams(vmem_limit_bytes=16 * MIB),
        cost_estimate=pl.CostEstimate(
            flops=2 * padded * count * width * (columns + ranks),
            bytes_accessed=width * (columns + 2 * ranks) * 2,
            transcendentals=0,
        ),
        name="block_products",
    )(row_place, *blocks, base_low, base_high, down, up, *before)


def others(received, before):
    count = len(received)

    def kernel(*refs):
        o_ref, sem = refs[-2], refs[-1]
        copies = [
            pltpu.make_async_copy(refs[i].at[1], o_ref.at[i], sem.at[i]) for i in range(count)
        ]
        for copy in copies:
            copy.start()
        for copy in copies:
            copy.wait()

    return pl.pallas_call(
        kernel,
        out_shape=jax.ShapeDtypeStruct((count,) + received[0].shape[1:], received[0].dtype),
        in_specs=[VMEM] * count + [ANY] * len(before),
        out_specs=VMEM,
        scratch_shapes=[pltpu.SemaphoreType.DMA((count,))],
        compiler_params=pltpu.CompilerParams(vmem_limit_bytes=8 * MIB),
        name="others",
    )(*received, *before)


def assemble(sources, row_place, received, adapters, rows):
    arrays = [array for array, _ in received]
    at_of = [(i, at) for i, (_, ats) in enumerate(received) for at in ats]
    count = len(at_of)
    pairs = rows // 2
    columns = arrays[0].shape[-1]
    slots = OWNER_ROW_LIMIT * count

    def kernel(place_ref, *refs):
        me = lax.axis_index("owner")
        source = [device_of(count // 2, me, what) for what in sources]
        o_ref, delta_ref, row_ref, out_sem = refs[-4:]
        piece_refs = [refs[i].at[at] for i, at in at_of]
        for a, ref in enumerate(piece_refs):
            delta_ref[:, a] = ref[pairs:]
        place = place_ref[pl.ds(me, 1), :]
        owner = place // (adapters * OWNER_ROW_LIMIT)
        place = place % OWNER_ROW_LIMIT
        slot = lax.broadcasted_iota(jnp.int32, (slots, rows), 0)
        piece, second = slot // OWNER_ROW_LIMIT, slot % OWNER_ROW_LIMIT
        match = jnp.zeros((slots, rows), jnp.float32)
        for a in range(count):
            match = jnp.where(
                (piece == a) & (owner == source[a]) & (place == second), 1.0, match
            )
        pick = match.T.astype(jnp.bfloat16)
        outs = []
        for a, ref in enumerate(piece_refs):
            delta = jnp.dot(
                pick,
                delta_ref[source[a]].reshape(slots, columns),
                preferred_element_type=jnp.float32,
            )
            base = ref[:pairs].reshape(rows, columns).astype(jnp.float32)
            row_ref[a] = (base + adapter_scale * delta).astype(row_ref.dtype)
            span = pl.ds(pl.multiple_of(source[a] * columns, columns), columns)
            outs.append(pltpu.make_async_copy(row_ref.at[a], o_ref.at[:, span], out_sem.at[a]))
            outs[-1].start()
        for copy in outs:
            copy.wait()

    return pl.pallas_call(
        kernel,
        out_shape=jax.ShapeDtypeStruct((rows, count * columns), jnp.bfloat16),
        in_specs=[VMEM] * (len(arrays) + 1),
        out_specs=ANY,
        scratch_shapes=[
            pltpu.VMEM((count, count, 2, columns), jnp.bfloat16),
            pltpu.VMEM((count, rows, columns), jnp.bfloat16),
            pltpu.SemaphoreType.DMA((count,)),
        ],
        compiler_params=pltpu.CompilerParams(vmem_limit_bytes=16 * MIB),
        name="assemble",
    )(row_place, *arrays)


def per_device(
    states, row_adapter_index, adapter_storage_slot, base_weight, down_weight, up_weight
):
    owner_count = lax.axis_size("owner")
    rows, width = states.shape
    adapters, rank = down_weight.shape[0], down_weight.shape[2]
    turned, swap, block_from, piece_from = ring_tables(owner_count)
    send = functools.partial(lax.ppermute, axis_name="owner")

    down = down_weight.transpose(0, 2, 1).reshape(adapters * rank, width)
    up = up_weight.reshape(adapters * rank, width)

    row_place = row_places(row_adapter_index, adapter_storage_slot, rows, adapters)
    chips = owner_count // 2
    last = chips // 2
    split = [list(range(at - 1, at + 1)) for at in range(last, 2, -2)][::-1]
    split = [list(range(1, split[0][0] if split else last + 1))] + split
    order, at = [], 2
    for hops in split:
        came = sum(2 if 2 * hop < chips else 1 for hop in hops)
        firsts, seconds = ([at + 2 * i + core for i in range(came)] for core in range(2))
        at += 2 * came
        if hops is split[-1]:
            firsts, seconds = firsts + [0], seconds + [1]
        order += firsts + seconds
    piece_from = [piece_from[i] for i in order]

    base_weight, down, up = (
        pltpu.with_memory_space_constraint(w, pltpu.HBM) for w in (base_weight, down, up)
    )
    own = pair_rows(states)
    first, second = own, send(own, perm=swap)
    groups = [[first, second]]
    held = [None] * 4
    received = []

    def products(hops, start, before, joined=False):
        blocks, places, result = [], [], 0
        for hop in hops:
            blocks += groups[hop]
            if len(groups[hop]) == 4:
                places += [(result, 0), (result + 1, 1), (result, 1), (result + 1, 0)]
                result += 2
            else:
                places += [(result, 0), (result, 1)]
                result += 1
        out = block_products(
            block_from[start : start + len(blocks)],
            row_place,
            blocks,
            places,
            held,
            rank,
            owner_count,
            before,
        )
        came, at = [], 0
        for hop in hops:
            came.append(send(out[at], perm=turned(-hop)) if hop else out[at])
            at += 1
            if len(groups[hop]) == 4:
                came.append(send(out[at], perm=turned(hop)))
                at += 1
        if joined:
            received[-1] += came
        else:
            received.append(came)
        return len(blocks), out[0]

    done = 2
    for hops in range(1, last + 1):
        first = send(first, perm=turned(1))
        if hops == 1:
            held[0], first = hold(base_weight, first, [row_place], half=0)
        if hops == 2:
            held[3], first = hold(up, first, [])
        if hops == last and len(split) > 1:
            for early in split[:-1]:
                count, made = products(early, done, [second])
                done += count
            first = after(first, [made])
        group = [first, send(first, perm=swap)]
        if 2 * hops < chips:
            second = send(second, perm=turned(1))
            if hops == 1:
                held[1], second = hold(base_weight, second, [], half=1)
            if hops == 2:
                held[2], second = hold(down, second, [], turn=True)
            group += [second, send(second, perm=swap)]
        groups.append(group)
    for i, (weight, how) in enumerate(
        [(base_weight, dict(half=0)), (base_weight, dict(half=1)), (down, dict(turn=True)), (up, {})]
    ):
        if held[i] is None:
            held[i], row_place = hold(weight, row_place, [], **how)
    _, made = products(split[-1], done, [])
    products([0], 0, [made], joined=True)
    arrays = []
    for came in received:
        passed = send(others(came, [made]), perm=swap)
        arrays += [(array, (0,)) for array in came] + [(passed, tuple(range(len(came))))]
    return assemble(piece_from, row_place, arrays, adapters, rows)


def solution(mesh):
    return jax.shard_map(
        per_device,
        mesh=mesh,
        in_specs=(
            P(("groups", "owner"), None),
            P("groups"),
            P("groups"),
            P(None, "owner"),
            P("owner", None, None),
            P("owner", None, None),
        ),
        out_specs=P(("groups", "owner"), None),
        check_vma=False,
    )
```
